256 devices in a mesh: tiles: 64 (over x, y_lo, z), fblk: 4 (over y_hi, core).
Axes of the slice: x: 4, y: 4 (y_hi: 2, y_lo: 2; y = y_hi * 2 + y_lo), z: 8, core: 2. Of those that a mesh axis runs over, the one named last changes fastest.
Arguments:
- images: float32 [64, 48, 128], P('tiles'), may hold values from -6 to 6
- sparse_codes: bfloat16 [64, 256, 48, 128], P('tiles', 'fblk'), may hold values from -0.5 to 0.5
- filters: float32 [256, 11, 11], P('fblk'), may hold values from -0.5 to 0.5
- plan: int32 [4], replicated, may hold values from 0 to 3, as said below
Outputs:
- filters_out: float32 [256, 11, 11], P('fblk')
- codes_out: bfloat16 [64, 256, 48, 128], P('tiles', 'fblk')
The draws below stay inside these ranges and needn't reach their ends.
Inputs may be any that keep to these rules, and one draw needn't show every extreme that they name: `plan`: names every filter block exactly once, in some order.
All inputs are finite; a program needn't handle non-finite values.
Results may differ from the reference program's by a relative error of at most 0.01.
Values sent between devices are 32-bit elements; how exact they have to be, the bound alone decides.
A program may use at most 64 MiB of HBM per device.

```python
import jax
import jax.numpy as jnp
from jax import lax

K = 256
TAPS = 11
H = 48
W = 128
STEPS = 4
KB = 64
TILES = 64
N_FBLK = 4


def draw_plan(key, part):
    order = jax.random.permutation(jax.random.fold_in(key, 17), N_FBLK)
    return order[:STEPS].astype(jnp.int32)


def levels(stream_key, dims, shards, least, high):
    level = 1.0
    for axis_at, blocks in shards:
        heights = jax.random.uniform(jax.random.fold_in(jax.random.fold_in(stream_key, 6), axis_at), (blocks,), jnp.float32, least / len(shards), high / len(shards))
        level = level * jnp.repeat(jnp.exp(heights), dims[axis_at] // blocks).reshape((-1,) + (1,) * (len(dims) - 1 - axis_at))
    return level


def noise(rng, extent, width, limit, split=(), kind=jnp.bfloat16):
    values = jax.random.normal(rng, extent, jnp.float32) * width
    if len(split) > 0:
        values = levels(rng, extent, split, -0.22, 0.18) * values
    return jnp.clip(values, min=-limit, max=limit).astype(kind)


def setup_inputs(seed: int = 0) -> dict:
    keys = jax.random.split(jax.random.key(seed), 5)
    images = noise(keys[0], (TILES, H, W), 1.0, 6.0, ((0, 64),), jnp.float32)
    sparse_codes = noise(keys[1], (TILES, K, H, W), 0.0625, 0.5, ((0, 64), (1, 4)))
    filters = noise(keys[2], (K, TAPS, TAPS), (TAPS * TAPS) ** -0.5, 0.5, ((0, 4),), jnp.float32)
    plan = draw_plan(jax.random.fold_in(keys[4], 71), 0)
    return dict(images=images, sparse_codes=sparse_codes, filters=filters, plan=plan)


step_filter = 128.0
step_code = 0.05
shrink_level = 0.02

def spread_one(tap_maps, height, breadth):
    padded = jnp.pad(tap_maps, ((0, 0), (5, 5), (5, 5)))
    summed = jnp.zeros((height, breadth), jnp.float32)
    for row_tap in range(11):
        for col_tap in range(11):
            summed = summed + padded[row_tap * 11 + col_tap, row_tap:row_tap + height, col_tap:col_tap + breadth]
    return summed

def shifted_one(resid):
    height, breadth = resid.shape
    padded = jnp.pad(resid, ((5, 5), (5, 5)))
    pieces = []
    for row_tap in range(11):
        for col_tap in range(11):
            pieces.append(padded[10 - row_tap:10 - row_tap + height, 10 - col_tap:10 - col_tap + breadth])
    return jnp.stack(pieces, axis=0).astype(jnp.bfloat16)

def synth_one(weights_bf, codes_tile):
    channels, height, breadth = codes_tile.shape
    tap_maps = jnp.dot(weights_bf.T, codes_tile.reshape(channels, height * breadth), preferred_element_type=jnp.float32)
    return spread_one(tap_maps.reshape(121, height, breadth), height, breadth)

def renorm(values):
    return values / jnp.sqrt(lax.optimization_barrier(jnp.sum(values * values, axis=1, keepdims=True)) + 1e-06)

def reference(images, sparse_codes, filters, plan):
    flat_filters = filters.reshape(K, 121)
    codes_now = sparse_codes
    pixels = float(TILES * H * W)
    for step_index in range(STEPS):
        block_id = plan[step_index]
        weights_bf = flat_filters.astype(jnp.bfloat16)
        residual = lax.map(lambda paired: synth_one(weights_bf, paired[0]) - paired[1], (codes_now, images))

        def tile_grad(paired):
            chosen = lax.dynamic_slice_in_dim(paired[0], block_id * KB, KB, 0)
            return jnp.dot(chosen.reshape(KB, -1), shifted_one(paired[1]).reshape(121, -1).T, preferred_element_type=jnp.float32)
        gradient = lax.optimization_barrier(jnp.sum(lax.map(tile_grad, (codes_now, residual)), axis=0))
        previous = lax.dynamic_slice_in_dim(flat_filters, block_id * KB, KB, 0)
        renewed = renorm(previous - step_filter * gradient / pixels)
        flat_filters = lax.dynamic_update_slice_in_dim(flat_filters, renewed, block_id * KB, 0)
        new_bf = flat_filters.astype(jnp.bfloat16)

        def tile_code(paired):
            resid = synth_one(new_bf, paired[0]) - paired[1]
            grad_code = jnp.dot(new_bf, shifted_one(resid).reshape(121, -1), preferred_element_type=jnp.float32)
            moved = paired[0].astype(jnp.float32) - step_code * grad_code.reshape(paired[0].shape)
            return (moved - jnp.clip(moved, -shrink_level, shrink_level)).astype(jnp.bfloat16)
        codes_now = lax.map(tile_code, (codes_now, images))
    return (flat_filters.reshape(K, 11, 11), codes_now)
```

```python
import jax
import jax.numpy as jnp
from jax import lax
from jax.experimental import pallas as pl
from jax.experimental.pallas import tpu as pltpu
from jax.sharding import PartitionSpec as P

STEPS = 4
TAPS = 11
H, W = 48, 128
PIX = H * W
KB = 64
HALF = KB // 2
COLS = 16 * TAPS
PAD = 5 * W
CODE_LANES = 60 * W
SHIFT_LANES = PIX + 2 * PAD
GROUPS = 3
MAP_LANES = 56 * W
CHUNK = 512
ROWS = CHUNK // W

step_filter = 128.0
step_code = 0.05
shrink_level = 0.02
MESH = pl.DeviceIdType.MESH
F32, BF16 = jnp.float32, jnp.bfloat16


def flip(index, mask):
    out = index
    bit = 1
    while bit <= mask:
        if mask & bit:
            out = out + bit * (1 - 2 * ((index // bit) % 2))
        bit *= 2
    return out


def tree_sum(parts):
    while len(parts) > 1:
        parts = [
            parts[i] + parts[i + 1] if i + 1 < len(parts) else parts[i]
            for i in range(0, len(parts), 2)
        ]
    return parts[0]


def nt_dot(a, b):
    return lax.dot_general(a, b, (((1,), (1,)), ((), ())), preferred_element_type=F32)


def kernel(
    plan, images, codes, filters, filters_out, codes_out,
    natural, held, maps, spread_mat, expand_mat, shifts, bank, parts, near, far, send, recv,
):
    tile, fblk = lax.axis_index("tiles"), lax.axis_index("fblk")
    z_peers = [(n, 0) for n in range(1, 8)]
    xy_peers = [(8 * n, 0) for n in range(1, 8)]
    group_peers = [(0, r) for r in range(1, 4)]
    peers = z_peers + xy_peers + group_peers

    def device(peer):
        return (flip(tile, peer[0]), flip(fblk, peer[1]))

    barrier = pltpu.get_barrier_semaphore()
    for peer in peers:
        pl.semaphore_signal(barrier, inc=1, device_id=device(peer), device_id_type=MESH)

    row = lax.broadcasted_iota(jnp.int32, (4 * GROUPS * 16, 128), 0)
    col = lax.broadcasted_iota(jnp.int32, (4 * GROUPS * 16, 128), 1)
    tap = (row + 5) & 15
    for r in range(4):
        first = r * GROUPS * 16
        line = ((row - first) >> 4) * 4 + r
        part = (tap < TAPS) & (line < TAPS) & (line * TAPS + 10 - tap == col)
        spread_mat[first : first + GROUPS * 16, :] = jnp.where(part, 1.0, 0.0).astype(BF16)[
            first : first + GROUPS * 16
        ]
    col = lax.broadcasted_iota(jnp.int32, (128, COLS), 0)
    row = lax.broadcasted_iota(jnp.int32, (128, COLS), 1)
    tap = (row + 5) & 15
    part = (tap < TAPS) & ((row >> 4) * TAPS + tap == col)
    expand_mat[...] = jnp.where(part, 1.0, 0.0).astype(BF16)
    held[:, 0:PAD] = jnp.zeros((KB, PAD), BF16)
    held[:, PAD + PIX : CODE_LANES] = jnp.zeros((KB, CODE_LANES - PAD - PIX), BF16)
    shifts[:, 0:PAD] = jnp.zeros((16, PAD), BF16)
    shifts[:, PAD + PIX : SHIFT_LANES] = jnp.zeros((16, PAD), BF16)
    bank[...] = filters[...]

    def unfold(k, carry):
        rows = pl.ds(pl.multiple_of(k * 8 * H, 8 * H), 8 * H)
        natural[rows, :] = codes[rows, :].astype(F32)
        return carry

    lax.fori_loop(0, KB // 8, unfold, 0)
    for y in range(H):
        held[:, PAD + y * W : PAD + (y + 1) * W] = natural[pl.ds(y, KB, stride=H), :].astype(BF16)

    tap = (lax.broadcasted_iota(jnp.int32, (16, W), 0) + 5) & 15
    lane = lax.broadcasted_iota(jnp.int32, (16, W), 1)
    source = lane - tap + 5
    inside = (tap < TAPS) & (source >= 0) & (source < W)

    def turn(front, back):
        front = pltpu.roll(front, 0, 1, stride=1, stride_axis=0)
        back = pltpu.roll(back, W - 8, 1, stride=1, stride_axis=0)
        return jnp.where(inside, jnp.concatenate([front, back], axis=0), 0.0)

    def synth(kind, s):
        @pl.when(tile >= 0)
        def _():
            slabs = nt_dot(spread_mat[...], bank[...].astype(BF16))
            weights = jnp.concatenate(
                [slabs[r * GROUPS * 16 : (r + 1) * GROUPS * 16] for r in range(4)], axis=1
            ).astype(BF16)
            lag = 3
            for c in range(H // ROWS + lag):
                at = c * CHUNK
                if at < MAP_LANES:
                    piled = jnp.concatenate(
                        [held[:, at + r * W : at + r * W + CHUNK] for r in range(4)], axis=0
                    )
                    maps[:, at : at + CHUNK] = jnp.dot(weights, piled, preferred_element_type=F32)
                if c >= lag:
                    for y in range((c - lag) * ROWS, (c - lag + 1) * ROWS):
                        total = tree_sum([
                            maps[g * 16 : (g + 1) * 16, (y + 4 * g) * W : (y + 4 * g + 1) * W]
                            for g in range(GROUPS)
                        ])
                        turned = turn(total[0:8], total[8:16])
                        parts[kind, s, 0, y : y + 1, :] = jnp.sum(turned, axis=0, keepdims=True)

    def copies(src, dst, q, s, n, peer):
        return pltpu.make_async_remote_copy(
            src_ref=src.at[s, 0], dst_ref=dst.at[s, n],
            send_sem=send.at[q, s], recv_sem=recv.at[q, s],
            device_id=device(peer), device_id_type=MESH,
        )

    def start(ref, q, s, targets):
        for n, peer in enumerate(targets):
            copies(ref, ref, q, s, n + 1, peer).start()

    def finish(ref, sem, q, s, count):
        got = ref.at[s, pl.ds(1, count)]
        pltpu.make_async_copy(got, got, sem.at[q, s]).wait()

    def exchange(kind, s):
        start(parts.at[kind], 4 + kind, s, group_peers)
        finish(parts.at[kind], recv, 4 + kind, s, 3)

        @pl.when(tile >= 0)
        def _():
            left = tree_sum([parts[kind, s, r] for r in range(4)]) - images[...]
            for y in range(H):
                line = jnp.broadcast_to(left[y : y + 1, :], (8, W))
                shifts[:, PAD + y * W : PAD + (y + 1) * W] = turn(line, line).astype(BF16)

        finish(parts.at[kind], send, 4 + kind, s, 3)

    def shift_rows(at):
        return jnp.concatenate(
            [shifts[:, at + (10 - a) * W : at + (10 - a) * W + CHUNK] for a in range(TAPS)], axis=0
        )

    def step(s, last):
        exchange(0, s)

        @pl.when(tile >= 0)
        def _():
            total = jnp.zeros((KB, COLS), F32)
            for c in range(PIX // CHUNK):
                at = c * CHUNK
                total = total + nt_dot(held[:, PAD + at : PAD + at + CHUNK], shift_rows(at))
            big = total.astype(BF16)
            rest = total - big.astype(F32)
            mid = rest.astype(BF16)
            small = (rest - mid.astype(F32)).astype(BF16)
            thirds = nt_dot(jnp.concatenate([big, mid, small], axis=0), expand_mat[...])
            total = thirds[0:KB] + (thirds[KB : 2 * KB] + thirds[2 * KB :])
            near[0, s, 0] = total[0:HALF]
            near[1, s, 0] = total[HALF:KB]

        start(near.at[0], 0, s, z_peers)
        start(near.at[1], 1, s, xy_peers)
        finish(near.at[0], recv, 0, s, 7)
        far[0, s, 0] = tree_sum([near[0, s, n] for n in range(8)])
        start(far.at[0], 2, s, xy_peers)
        finish(near.at[1], recv, 1, s, 7)
        far[1, s, 0] = tree_sum([near[1, s, n] for n in range(8)])
        start(far.at[1], 3, s, z_peers)
        for q in range(2):
            finish(near.at[q], send, q, s, 7)
        for q in range(2):
            finish(far.at[q], recv, 2 + q, s, 7)
        gradient = jnp.concatenate(
            [tree_sum([far[q, s, n] for n in range(8)]) for q in range(2)], axis=0
        )
        old = bank[...]
        values = old - step_filter * gradient / 393216.0
        values = values / jnp.sqrt(jnp.sum(values * values, axis=1, keepdims=True) + 1e-06)
        owner = jnp.full((KB, 128), plan[s], jnp.int32) == jnp.full((KB, 128), fblk, jnp.int32)
        bank[...] = jnp.where(owner, values, old)
        for q in range(2):
            finish(far.at[q], send, 2 + q, s, 7)
        synth(1, s)
        exchange(1, s)

        @pl.when(tile >= 0)
        def _():
            weights = jnp.dot(
                bank[...].astype(BF16), expand_mat[...], preferred_element_type=F32
            ).astype(BF16)
            for c in range(PIX // CHUNK):
                at = c * CHUNK
                slope = jnp.dot(weights, shift_rows(at), preferred_element_type=F32)
                value = held[:, PAD + at : PAD + at + CHUNK].astype(F32) - step_code * slope
                value = value - jnp.clip(value, -shrink_level, shrink_level)
                if last:
                    for i in range(ROWS):
                        natural[pl.ds(c * ROWS + i, KB, stride=H), :] = value[:, i * W : (i + 1) * W]
                else:
                    held[:, PAD + at : PAD + at + CHUNK] = value.astype(BF16)

        if not last:
            synth(0, s + 1)

    synth(0, 0)
    pl.semaphore_wait(barrier, len(peers))

    def early_step(s, carry):
        step(s, False)
        return carry

    lax.fori_loop(0, STEPS - 1, early_step, 0)
    step(STEPS - 1, True)
    filters_out[...] = bank[...]

    def fold(k, carry):
        rows = pl.ds(pl.multiple_of(k * 8 * H, 8 * H), 8 * H)
        codes_out[rows, :] = natural[rows, :].astype(BF16)
        return carry

    lax.fori_loop(0, KB // 8, fold, 0)


def body(images, sparse_codes, filters, plan):
    flat_filters = jnp.pad(filters.reshape(KB, 121), ((0, 0), (0, 7)))
    vmem = pl.BlockSpec(memory_space=pltpu.VMEM)
    new_filters, new_codes = pl.pallas_call(
        kernel,
        out_shape=(
            jax.ShapeDtypeStruct((KB, 128), F32),
            jax.ShapeDtypeStruct((KB * H, W), BF16),
        ),
        in_specs=[pl.BlockSpec(memory_space=pltpu.SMEM), vmem, vmem, vmem],
        out_specs=(vmem, vmem),
        scratch_shapes=[
            pltpu.VMEM((KB * H, W), F32),
            pltpu.VMEM((KB, CODE_LANES), BF16),
            pltpu.VMEM((GROUPS * 16, MAP_LANES), F32),
            pltpu.VMEM((4 * GROUPS * 16, 128), BF16),
            pltpu.VMEM((128, COLS), BF16),
            pltpu.VMEM((16, SHIFT_LANES), BF16),
            pltpu.VMEM((KB, 128), F32),
            pltpu.VMEM((2, STEPS, 4, H, W), F32),
            pltpu.VMEM((2, STEPS, 8, HALF, 128), F32),
            pltpu.VMEM((2, STEPS, 8, HALF, 128), F32),
            pltpu.SemaphoreType.DMA((6, STEPS)),
            pltpu.SemaphoreType.DMA((6, STEPS)),
        ],
        compiler_params=pltpu.CompilerParams(
            collective_id=0, has_side_effects=True, vmem_limit_bytes=40 * 1024 * 1024
        ),
        name="coordinate_steps",
    )(plan, images.reshape(H, W), sparse_codes.reshape(KB * H, W), flat_filters)
    return (
        new_filters[:, :121].reshape(KB, TAPS, TAPS),
        new_codes.reshape(1, KB, H, W),
    )


def solution(mesh):
    in_specs = (P("tiles", None, None), P("tiles", "fblk", None, None), P("fblk", None, None), P())
    out_specs = (P("fblk", None, None), P("tiles", "fblk", None, None))
    return jax.shard_map(body, mesh=mesh, in_specs=in_specs, out_specs=out_specs, check_vma=False)
```

```python
import jax
import jax.numpy as jnp
from jax import lax
from jax.experimental import pallas as pl
from jax.experimental.pallas import tpu as pltpu
from jax.sharding import PartitionSpec as P

STEPS = 4
TAPS = 11
H, W = 48, 128
PIX = H * W
KB = 64
HALF = KB // 2
COLS = 16 * TAPS
PAD = 5 * W
CODE_LANES = 60 * W
SHIFT_LANES = PIX + 2 * PAD
GROUPS = 3
MAP_LANES = 56 * W
CHUNK = 512
ROWS = CHUNK // W

step_filter = 128.0
step_code = 0.05
shrink_level = 0.02
MESH = pl.DeviceIdType.MESH
F32, BF16 = jnp.float32, jnp.bfloat16


def flip(index, mask):
    out = index
    bit = 1
    while bit <= mask:
        if mask & bit:
            out = out + bit * (1 - 2 * ((index // bit) % 2))
        bit *= 2
    return out


def tree_sum(parts):
    while len(parts) > 1:
        parts = [
            parts[i] + parts[i + 1] if i + 1 < len(parts) else parts[i]
            for i in range(0, len(parts), 2)
        ]
    return parts[0]


def nt_dot(a, b):
    return lax.dot_general(a, b, (((1,), (1,)), ((), ())), preferred_element_type=F32)


def kernel(
    plan, images_in, codes_in, filters_in, filters_out, codes_out,
    images, codes, filters, turned_filters, natural, held, maps, spread_mat, expand_mat, shifts, bank, parts, near, far, send, recv, local,
    synth_mat, code_mat,
):
    tile, fblk = lax.axis_index("tiles"), lax.axis_index("fblk")
    z_peers = [(n, 0) for n in range(1, 8)]
    xy_peers = [(8 * n, 0) for n in range(1, 8)]
    group_peers = [(0, r) for r in range(1, 4)]
    peers = z_peers + xy_peers + group_peers
    along_z = (z_peers, (4, 3, 5, 6, 2, 7, 1))
    along_xy = (xy_peers, (5, 4, 7, 3, 6, 2, 1))
    in_group = (group_peers, (2, 3, 1))

    places = {peer: (flip(tile, peer[0]), flip(fblk, peer[1])) for peer in peers}

    def device(peer):
        return places[peer]

    barrier = pltpu.get_barrier_semaphore()
    for peer in peers:
        pl.semaphore_signal(barrier, inc=1, device_id=device(peer), device_id_type=MESH)

    loads = [
        pltpu.make_async_copy(codes_in, codes, local.at[0]),
        pltpu.make_async_copy(filters_in, filters, local.at[1]),
        pltpu.make_async_copy(images_in, images, local.at[2]),
    ]
    for load in loads:
        load.start()

    row = lax.broadcasted_iota(jnp.int32, (4 * GROUPS * 16, 128), 0)
    col = lax.broadcasted_iota(jnp.int32, (4 * GROUPS * 16, 128), 1)
    tap = (row + 5) & 15
    for r in range(4):
        first = r * GROUPS * 16
        line = ((row - first) >> 4) * 4 + r
        part = (tap < TAPS) & (line < TAPS) & (line * TAPS + 10 - tap == col)
        spread_mat[first : first + GROUPS * 16, :] = jnp.where(part, 1.0, 0.0).astype(BF16)[
            first : first + GROUPS * 16
        ]
    col = lax.broadcasted_iota(jnp.int32, (128, COLS), 0)
    row = lax.broadcasted_iota(jnp.int32, (128, COLS), 1)
    tap = (row + 5) & 15
    part = (tap < TAPS) & ((row >> 4) * TAPS + tap == col)
    expand_mat[...] = jnp.where(part, 1.0, 0.0).astype(BF16)
    held[:, 0:PAD] = jnp.zeros((KB, PAD), BF16)
    held[:, PAD + PIX : CODE_LANES] = jnp.zeros((KB, CODE_LANES - PAD - PIX), BF16)
    shifts[:, 0:PAD] = jnp.zeros((16, PAD), BF16)
    shifts[:, PAD + PIX : SHIFT_LANES] = jnp.zeros((16, PAD), BF16)
    for load in loads:
        load.wait()
    turned_filters[...] = jnp.zeros((128, 128), F32)
    for a in range(TAPS):
        turned_filters[a * TAPS : (a + 1) * TAPS, 0:KB] = filters[a]
    bank[...] = jnp.transpose(turned_filters[...])[0:KB, :]

    def unfold(k, carry):
        rows = pl.ds(pl.multiple_of(k * 8 * H, 8 * H), 8 * H)
        natural[rows, :] = codes[rows, :].astype(F32)
        return carry

    lax.fori_loop(0, KB // 8, unfold, 0)
    for y in range(H):
        held[:, PAD + y * W : PAD + (y + 1) * W] = natural[pl.ds(y, KB, stride=H), :].astype(BF16)

    tap = (lax.broadcasted_iota(jnp.int32, (16, W), 0) + 5) & 15
    lane = lax.broadcasted_iota(jnp.int32, (16, W), 1)
    source = lane - tap + 5
    inside = (tap < TAPS) & (source >= 0) & (source < W)

    def turn(front, back):
        front = pltpu.roll(front, 0, 1, stride=1, stride_axis=0)
        back = pltpu.roll(back, W - 8, 1, stride=1, stride_axis=0)
        return jnp.where(inside, jnp.concatenate([front, back], axis=0), 0.0)

    def set_synth_mat():
        slabs = nt_dot(spread_mat[...], bank[...].astype(BF16))
        synth_mat[...] = jnp.concatenate(
            [slabs[r * GROUPS * 16 : (r + 1) * GROUPS * 16] for r in range(4)], axis=1
        ).astype(BF16)

    def synth(kind, s):
        @pl.when(tile >= 0)
        def _():
            weights = synth_mat[...]
            lag = 3
            for c in range(H // ROWS + lag):
                at = c * CHUNK
                if at < MAP_LANES:
                    piled = jnp.concatenate(
                        [held[:, at + r * W : at + r * W + CHUNK] for r in range(4)], axis=0
                    )
                    maps[:, at : at + CHUNK] = jnp.dot(weights, piled, preferred_element_type=F32)
                if c >= lag:
                    for y in range((c - lag) * ROWS, (c - lag + 1) * ROWS):
                        total = tree_sum([
                            maps[g * 16 : (g + 1) * 16, (y + 4 * g) * W : (y + 4 * g + 1) * W]
                            for g in range(GROUPS)
                        ])
                        turned = turn(total[0:8], total[8:16])
                        parts[kind, s, 0, y : y + 1, :] = jnp.sum(turned, axis=0, keepdims=True)

    def copies(src, dst, q, s, n, peer):
        return pltpu.make_async_remote_copy(
            src_ref=src.at[s, 0], dst_ref=dst.at[s, n],
            send_sem=send.at[q, s], recv_sem=recv.at[q, s],
            device_id=device(peer), device_id_type=MESH,
        )

    def start(ref, q, s, targets):
        for n in targets[1]:
            copies(ref, ref, q, s, n, targets[0][n - 1]).start()

    def finish(ref, sem, q, s, count):
        got = ref.at[s, pl.ds(1, count)]
        pltpu.make_async_copy(got, got, sem.at[q, s]).wait()

    def exchange(kind, s, meanwhile):
        start(parts.at[kind], 4 + kind, s, in_group)
        pl.when(tile >= 0)(meanwhile)
        finish(parts.at[kind], recv, 4 + kind, s, 3)

        @pl.when(tile >= 0)
        def _():
            left = tree_sum([parts[kind, s, r] for r in range(4)]) - images[...]
            for y in range(H):
                line = jnp.broadcast_to(left[y : y + 1, :], (8, W))
                shifts[:, PAD + y * W : PAD + (y + 1) * W] = turn(line, line).astype(BF16)


    def shift_rows(at):
        return jnp.concatenate(
            [shifts[:, at + (10 - a) * W : at + (10 - a) * W + CHUNK] for a in range(TAPS)], axis=0
        )

    def set_code_mat():
        code_mat[...] = jnp.dot(
            bank[...].astype(BF16), expand_mat[...], preferred_element_type=F32
        ).astype(BF16)

    def step(s, last):
        exchange(0, s, lambda: None)

        @pl.when(tile >= 0)
        def _():
            total = jnp.zeros((KB, COLS), F32)
            for c in range(PIX // CHUNK):
                at = c * CHUNK
                total = total + nt_dot(held[:, PAD + at : PAD + at + CHUNK], shift_rows(at))
            big = total.astype(BF16)
            rest = total - big.astype(F32)
            mid = rest.astype(BF16)
            small = (rest - mid.astype(F32)).astype(BF16)
            thirds = nt_dot(jnp.concatenate([big, mid, small], axis=0), expand_mat[...])
            total = thirds[0:KB] + (thirds[KB : 2 * KB] + thirds[2 * KB :])
            near[0, s, 0] = total[0:HALF]
            near[1, s, 0] = total[HALF:KB]

        start(near.at[0], 0, s, along_z)
        start(near.at[1], 1, s, along_xy)
        finish(near.at[1], recv, 1, s, 7)
        far[1, s, 0] = tree_sum([near[1, s, n] for n in range(8)])
        start(far.at[1], 3, s, along_z)
        finish(near.at[0], recv, 0, s, 7)
        far[0, s, 0] = tree_sum([near[0, s, n] for n in range(8)])
        start(far.at[0], 2, s, along_xy)
        for q in range(2):
            finish(far.at[q], recv, 2 + q, s, 7)
        gradient = jnp.concatenate(
            [tree_sum([far[q, s, n] for n in range(8)]) for q in range(2)], axis=0
        )
        old = bank[...]
        values = old - step_filter * gradient / 393216.0
        values = values / jnp.sqrt(jnp.sum(values * values, axis=1, keepdims=True) + 1e-06)
        owner = jnp.full((KB, 128), plan[s], jnp.int32) == jnp.full((KB, 128), fblk, jnp.int32)
        bank[...] = jnp.where(owner, values, old)
        set_synth_mat()
        synth(1, s)
        exchange(1, s, set_code_mat)

        @pl.when(tile >= 0)
        def _():
            weights = code_mat[...]
            for c in range(PIX // CHUNK):
                at = c * CHUNK
                slope = jnp.dot(weights, shift_rows(at), preferred_element_type=F32)
                value = held[:, PAD + at : PAD + at + CHUNK].astype(F32) - step_code * slope
                value = value - jnp.clip(value, -shrink_level, shrink_level)
                if last:
                    for i in range(ROWS):
                        natural[pl.ds(c * ROWS + i, KB, stride=H), :] = value[:, i * W : (i + 1) * W]
                else:
                    held[:, PAD + at : PAD + at + CHUNK] = value.astype(BF16)

        if not last:
            synth(0, s + 1)

    set_synth_mat()
    synth(0, 0)
    pl.semaphore_wait(barrier, len(peers))

    def early_step(s, carry):
        step(s, False)
        return carry

    lax.fori_loop(0, STEPS - 1, early_step, 0)
    step(STEPS - 1, True)
    for s in range(STEPS):
        for q in range(2):
            finish(near.at[q], send, q, s, 7)
            finish(far.at[q], send, 2 + q, s, 7)
            finish(parts.at[q], send, 4 + q, s, 3)
    turned_filters[0:KB, :] = bank[...]
    turned_filters[...] = jnp.transpose(turned_filters[...])
    for a in range(TAPS):
        filters_out[a] = turned_filters[a * TAPS : (a + 1) * TAPS, 0:KB]

    def fold(k, carry):
        rows = pl.ds(pl.multiple_of(k * 8 * H, 8 * H), 8 * H)
        codes_out[rows, :] = natural[rows, :].astype(BF16)
        return carry

    lax.fori_loop(0, KB // 8, fold, 0)


def body(images, sparse_codes, filters, plan):
    vmem = pl.BlockSpec(memory_space=pltpu.VMEM)
    hbm = pl.BlockSpec(memory_space=pltpu.HBM)
    new_filters, new_codes = pl.pallas_call(
        kernel,
        out_shape=(
            jax.ShapeDtypeStruct((TAPS, TAPS, KB), F32),
            jax.ShapeDtypeStruct((KB * H, W), BF16),
        ),
        in_specs=[pl.BlockSpec(memory_space=pltpu.SMEM), hbm, hbm, hbm],
        out_specs=(vmem, vmem),
        scratch_shapes=[
            pltpu.VMEM((H, W), F32),
            pltpu.VMEM((KB * H, W), BF16),
            pltpu.VMEM((TAPS, TAPS, KB), F32),
            pltpu.VMEM((128, 128), F32),
            pltpu.VMEM((KB * H, W), F32),
            pltpu.VMEM((KB, CODE_LANES), BF16),
            pltpu.VMEM((GROUPS * 16, MAP_LANES), F32),
            pltpu.VMEM((4 * GROUPS * 16, 128), BF16),
            pltpu.VMEM((128, COLS), BF16),
            pltpu.VMEM((16, SHIFT_LANES), BF16),
            pltpu.VMEM((KB, 128), F32),
            pltpu.VMEM((2, STEPS, 4, H, W), F32),
            pltpu.VMEM((2, STEPS, 8, HALF, 128), F32),
            pltpu.VMEM((2, STEPS, 8, HALF, 128), F32),
            pltpu.SemaphoreType.DMA((6, STEPS)),
            pltpu.SemaphoreType.DMA((6, STEPS)),
            pltpu.SemaphoreType.DMA((3,)),
            pltpu.VMEM((GROUPS * 16, 4 * KB), BF16),
            pltpu.VMEM((KB, COLS), BF16),
        ],
        compiler_params=pltpu.CompilerParams(
            collective_id=0, has_side_effects=True, vmem_limit_bytes=52 * 1024 * 1024 + 512 * 1024
        ),
        name="coordinate_steps",
    )(plan, images.reshape(H, W), sparse_codes.reshape(KB * H, W), filters.transpose(1, 2, 0))
    return (
        new_filters.transpose(2, 0, 1),
        new_codes.reshape(1, KB, H, W),
    )


def solution(mesh):
    in_specs = (P("tiles", None, None), P("tiles", "fblk", None, None), P("fblk", None, None), P())
    out_specs = (P("fblk", None, None), P("tiles", "fblk", None, None))
    return jax.shard_map(body, mesh=mesh, in_specs=in_specs, out_specs=out_specs, check_vma=False)
```

```python
import jax
import jax.numpy as jnp
from jax import lax
from jax.experimental import pallas as pl
from jax.experimental.pallas import tpu as pltpu
from jax.sharding import PartitionSpec as P

STEPS = 4
TAPS = 11
H, W = 48, 128
PIX = H * W
KB = 64
HALF = KB // 2
COLS = 16 * TAPS
PAD = 5 * W
CODE_LANES = 60 * W
SHIFT_LANES = PIX + 2 * PAD
GROUPS = 3
MAP_LANES = 56 * W
CHUNK = 512
ROWS = CHUNK // W
UPPER = H // 2
EARLY = (UPPER - 5) // ROWS

step_filter = 128.0
step_code = 0.05
shrink_level = 0.02
MESH = pl.DeviceIdType.MESH
F32, BF16 = jnp.float32, jnp.bfloat16


def flip(index, mask):
    out = index
    bit = 1
    while bit <= mask:
        if mask & bit:
            out = out + bit * (1 - 2 * ((index // bit) % 2))
        bit *= 2
    return out


def tree_sum(parts):
    while len(parts) > 1:
        parts = [
            parts[i] + parts[i + 1] if i + 1 < len(parts) else parts[i]
            for i in range(0, len(parts), 2)
        ]
    return parts[0]


def nt_dot(a, b):
    return lax.dot_general(a, b, (((1,), (1,)), ((), ())), preferred_element_type=F32)


def kernel(
    plan, images_in, codes_in, filters_in, filters_out, codes_out,
    images, codes, filters, turned_filters, natural, held, maps, spread_mat, expand_mat, shifts, bank, parts, near, far, send, recv, local,
    synth_mat, code_mat, early_grad,
):
    tile, fblk = lax.axis_index("tiles"), lax.axis_index("fblk")
    z_peers = [(n, 0) for n in range(1, 8)]
    xy_peers = [(8 * n, 0) for n in range(1, 8)]
    group_peers = [(0, r) for r in range(1, 4)]
    peers = z_peers + xy_peers + group_peers
    along_z = (z_peers, (4, 3, 5, 6, 2, 7, 1))
    along_xy = (xy_peers, (5, 4, 7, 3, 6, 2, 1))
    in_group = (group_peers, (2, 3, 1))

    farthest_first = [
        group[n - 1] for group, n in [(z_peers, n) for n in along_z[1]] + [(xy_peers, n) for n in along_xy[1]]
        + [(group_peers, n) for n in in_group[1]]
    ]
    places = {peer: (flip(tile, peer[0]), flip(fblk, peer[1])) for peer in peers}

    def device(peer):
        return places[peer]

    barrier = pltpu.get_barrier_semaphore()
    for peer in farthest_first:
        pl.semaphore_signal(barrier, inc=1, device_id=device(peer), device_id_type=MESH)

    loads = [
        pltpu.make_async_copy(codes_in, codes, local.at[0]),
        pltpu.make_async_copy(filters_in, filters, local.at[1]),
        pltpu.make_async_copy(images_in, images, local.at[2]),
    ]
    for load in loads:
        load.start()

    row = lax.broadcasted_iota(jnp.int32, (4 * GROUPS * 16, 128), 0)
    col = lax.broadcasted_iota(jnp.int32, (4 * GROUPS * 16, 128), 1)
    tap = (row + 5) & 15
    for r in range(4):
        first = r * GROUPS * 16
        line = ((row - first) >> 4) * 4 + r
        part = (tap < TAPS) & (line < TAPS) & (line * TAPS + 10 - tap == col)
        spread_mat[first : first + GROUPS * 16, :] = jnp.where(part, 1.0, 0.0).astype(BF16)[
            first : first + GROUPS * 16
        ]
    col = lax.broadcasted_iota(jnp.int32, (128, COLS), 0)
    row = lax.broadcasted_iota(jnp.int32, (128, COLS), 1)
    tap = (row + 5) & 15
    part = (tap < TAPS) & ((row >> 4) * TAPS + tap == col)
    expand_mat[...] = jnp.where(part, 1.0, 0.0).astype(BF16)
    held[:, 0:PAD] = jnp.zeros((KB, PAD), BF16)
    held[:, PAD + PIX : CODE_LANES] = jnp.zeros((KB, CODE_LANES - PAD - PIX), BF16)
    shifts[:, 0:PAD] = jnp.zeros((16, PAD), BF16)
    shifts[:, PAD + PIX : SHIFT_LANES] = jnp.zeros((16, PAD), BF16)
    for load in loads:
        load.wait()
    turned_filters[...] = jnp.zeros((128, 128), F32)
    for a in range(TAPS):
        turned_filters[a * TAPS : (a + 1) * TAPS, 0:KB] = filters[a]
    bank[...] = jnp.transpose(turned_filters[...])[0:KB, :]

    def unfold(k, carry):
        rows = pl.ds(pl.multiple_of(k * 8 * H, 8 * H), 8 * H)
        natural[rows, :] = codes[rows, :].astype(F32)
        return carry

    lax.fori_loop(0, KB // 8, unfold, 0)
    for y in range(H):
        held[:, PAD + y * W : PAD + (y + 1) * W] = natural[pl.ds(y, KB, stride=H), :].astype(BF16)

    tap = (lax.broadcasted_iota(jnp.int32, (16, W), 0) + 5) & 15
    lane = lax.broadcasted_iota(jnp.int32, (16, W), 1)
    source = lane - tap + 5
    inside = (tap < TAPS) & (source >= 0) & (source < W)

    def turn(front, back):
        front = pltpu.roll(front, 0, 1, stride=1, stride_axis=0)
        back = pltpu.roll(back, W - 8, 1, stride=1, stride_axis=0)
        return jnp.where(inside, jnp.concatenate([front, back], axis=0), 0.0)

    def set_synth_mat():
        slabs = nt_dot(spread_mat[...], bank[...].astype(BF16))
        synth_mat[...] = jnp.concatenate(
            [slabs[r * GROUPS * 16 : (r + 1) * GROUPS * 16] for r in range(4)], axis=1
        ).astype(BF16)

    def synth(kind, s, half):
        @pl.when(tile >= 0)
        def _():
            weights = synth_mat[...]
            lag = 3
            middle, end = UPPER // ROWS + lag, H // ROWS + lag
            for c in range(middle) if half == 0 else range(middle, end):
                at = c * CHUNK
                if at < MAP_LANES:
                    piled = jnp.concatenate(
                        [held[:, at + r * W : at + r * W + CHUNK] for r in range(4)], axis=0
                    )
                    maps[:, at : at + CHUNK] = jnp.dot(weights, piled, preferred_element_type=F32)
                if c >= lag:
                    for y in range((c - lag) * ROWS, (c - lag + 1) * ROWS):
                        total = tree_sum([
                            maps[g * 16 : (g + 1) * 16, (y + 4 * g) * W : (y + 4 * g + 1) * W]
                            for g in range(GROUPS)
                        ])
                        turned = turn(total[0:8], total[8:16])
                        parts[kind, s, 0, y : y + 1, :] = jnp.sum(turned, axis=0, keepdims=True)

    def copies(src, dst, q, s, n, peer):
        return pltpu.make_async_remote_copy(
            src_ref=src.at[s, 0], dst_ref=dst.at[s, n],
            send_sem=send.at[q, s], recv_sem=recv.at[q, s],
            device_id=device(peer), device_id_type=MESH,
        )

    def start(ref, q, s, targets):
        for n in targets[1]:
            copies(ref, ref, q, s, n, targets[0][n - 1]).start()

    def finish(ref, sem, q, s, count):
        got = ref.at[s, pl.ds(1, count)]
        pltpu.make_async_copy(got, got, sem.at[q, s]).wait()

    def send_parts(kind, s, half):
        rows = pl.ds(half * UPPER, UPPER)
        for n in in_group[1]:
            pltpu.make_async_remote_copy(
                src_ref=parts.at[kind, s, 0, rows], dst_ref=parts.at[kind, s, n, rows],
                send_sem=send.at[4 + 2 * kind + half, s], recv_sem=recv.at[4 + 2 * kind + half, s],
                device_id=device(group_peers[n - 1]), device_id_type=MESH,
            ).start()

    def finish_parts(sem, kind, s, half):
        got = parts.at[kind, s, pl.ds(1, 3), pl.ds(half * UPPER, UPPER)]
        pltpu.make_async_copy(got, got, sem.at[4 + 2 * kind + half, s]).wait()

    def synth_and_send(kind, s):
        for half in range(2):
            synth(kind, s, half)
            send_parts(kind, s, half)

    def exchange(kind, s, work):
        for half in range(2):
            finish_parts(recv, kind, s, half)

            @pl.when(tile >= 0)
            def _():
                first = half * UPPER
                rows = slice(first, first + UPPER)
                left = tree_sum([parts[kind, s, r, rows] for r in range(4)]) - images[rows, :]
                for y in range(UPPER):
                    line = jnp.broadcast_to(left[y : y + 1, :], (8, W))
                    at = PAD + (first + y) * W
                    shifts[:, at : at + W] = turn(line, line).astype(BF16)
                work(half, range(EARLY) if half == 0 else range(EARLY, PIX // CHUNK))

    def shift_rows(at):
        return jnp.concatenate(
            [shifts[:, at + (10 - a) * W : at + (10 - a) * W + CHUNK] for a in range(TAPS)], axis=0
        )

    def set_code_mat():
        code_mat[...] = jnp.dot(
            bank[...].astype(BF16), expand_mat[...], preferred_element_type=F32
        ).astype(BF16)

    def step(s, last):
        def to_gradient(half, chunks):
            total = jnp.zeros((KB, COLS), F32) if half == 0 else early_grad[...]
            for c in chunks:
                at = c * CHUNK
                total = total + nt_dot(held[:, PAD + at : PAD + at + CHUNK], shift_rows(at))
            if half == 0:
                early_grad[...] = total
                return
            big = total.astype(BF16)
            rest = total - big.astype(F32)
            mid = rest.astype(BF16)
            small = (rest - mid.astype(F32)).astype(BF16)
            for q in range(2):
                part = slice(q * HALF, (q + 1) * HALF)
                thirds = nt_dot(
                    jnp.concatenate([big[part], mid[part], small[part]], axis=0), expand_mat[...]
                )
                near[q, s, 0] = thirds[0:HALF] + (thirds[HALF : 2 * HALF] + thirds[2 * HALF :])
                start(near.at[q], q, s, (along_z, along_xy)[q])

        exchange(0, s, to_gradient)

        finish(near.at[1], recv, 1, s, 7)
        far[1, s, 0] = tree_sum([near[1, s, n] for n in range(8)])
        start(far.at[1], 3, s, along_z)
        finish(near.at[0], recv, 0, s, 7)
        far[0, s, 0] = tree_sum([near[0, s, n] for n in range(8)])
        start(far.at[0], 2, s, along_xy)
        for q in range(2):
            finish(far.at[q], recv, 2 + q, s, 7)
        gradient = jnp.concatenate(
            [tree_sum([far[q, s, n] for n in range(8)]) for q in range(2)], axis=0
        )
        old = bank[...]
        values = old - step_filter * gradient / 393216.0
        values = values / jnp.sqrt(jnp.sum(values * values, axis=1, keepdims=True) + 1e-06)
        owner = jnp.full((KB, 128), plan[s], jnp.int32) == jnp.full((KB, 128), fblk, jnp.int32)
        bank[...] = jnp.where(owner, values, old)
        set_synth_mat()
        synth_and_send(1, s)
        pl.when(tile >= 0)(set_code_mat)

        def to_codes(half, chunks):
            weights = code_mat[...]
            for c in chunks:
                at = c * CHUNK
                slope = jnp.dot(weights, shift_rows(at), preferred_element_type=F32)
                value = held[:, PAD + at : PAD + at + CHUNK].astype(F32) - step_code * slope
                value = value - jnp.clip(value, -shrink_level, shrink_level)
                if last:
                    for i in range(ROWS):
                        natural[pl.ds(c * ROWS + i, KB, stride=H), :] = value[:, i * W : (i + 1) * W]
                else:
                    held[:, PAD + at : PAD + at + CHUNK] = value.astype(BF16)

        exchange(1, s, to_codes)
        if not last:
            synth_and_send(0, s + 1)

    set_synth_mat()
    for half in range(2):
        synth(0, 0, half)
    pl.semaphore_wait(barrier, len(peers))
    for half in range(2):
        send_parts(0, 0, half)

    def early_step(s, carry):
        step(s, False)
        return carry

    lax.fori_loop(0, STEPS - 1, early_step, 0)
    step(STEPS - 1, True)
    for s in range(STEPS):
        for q in range(2):
            finish(near.at[q], send, q, s, 7)
            finish(far.at[q], send, 2 + q, s, 7)
            for half in range(2):
                finish_parts(send, q, s, half)
    turned_filters[0:KB, :] = bank[...]
    turned_filters[...] = jnp.transpose(turned_filters[...])
    for a in range(TAPS):
        filters_out[a] = turned_filters[a * TAPS : (a + 1) * TAPS, 0:KB]

    def fold(k, carry):
        rows = pl.ds(pl.multiple_of(k * 8 * H, 8 * H), 8 * H)
        codes_out[rows, :] = natural[rows, :].astype(BF16)
        return carry

    lax.fori_loop(0, KB // 8, fold, 0)


def body(images, sparse_codes, filters, plan):
    vmem = pl.BlockSpec(memory_space=pltpu.VMEM)
    hbm = pl.BlockSpec(memory_space=pltpu.HBM)
    new_filters, new_codes = pl.pallas_call(
        kernel,
        out_shape=(
            jax.ShapeDtypeStruct((TAPS, TAPS, KB), F32),
            jax.ShapeDtypeStruct((KB * H, W), BF16),
        ),
        in_specs=[pl.BlockSpec(memory_space=pltpu.SMEM), hbm, hbm, hbm],
        out_specs=(vmem, vmem),
        scratch_shapes=[
            pltpu.VMEM((H, W), F32),
            pltpu.VMEM((KB * H, W), BF16),
            pltpu.VMEM((TAPS, TAPS, KB), F32),
            pltpu.VMEM((128, 128), F32),
            pltpu.VMEM((KB * H, W), F32),
            pltpu.VMEM((KB, CODE_LANES), BF16),
            pltpu.VMEM((GROUPS * 16, MAP_LANES), F32),
            pltpu.VMEM((4 * GROUPS * 16, 128), BF16),
            pltpu.VMEM((128, COLS), BF16),
            pltpu.VMEM((16, SHIFT_LANES), BF16),
            pltpu.VMEM((KB, 128), F32),
            pltpu.VMEM((2, STEPS, 4, H, W), F32),
            pltpu.VMEM((2, STEPS, 8, HALF, 128), F32),
            pltpu.VMEM((2, STEPS, 8, HALF, 128), F32),
            pltpu.SemaphoreType.DMA((8, STEPS)),
            pltpu.SemaphoreType.DMA((8, STEPS)),
            pltpu.SemaphoreType.DMA((3,)),
            pltpu.VMEM((GROUPS * 16, 4 * KB), BF16),
            pltpu.VMEM((KB, COLS), BF16),
            pltpu.VMEM((KB, COLS), F32),
        ],
        compiler_params=pltpu.CompilerParams(
            collective_id=0, has_side_effects=True, vmem_limit_bytes=52 * 1024 * 1024 + 512 * 1024
        ),
        name="coordinate_steps",
    )(plan, images.reshape(H, W), sparse_codes.reshape(KB * H, W), filters.transpose(1, 2, 0))
    return (
        new_filters.transpose(2, 0, 1),
        new_codes.reshape(1, KB, H, W),
    )


def solution(mesh):
    in_specs = (P("tiles", None, None), P("tiles", "fblk", None, None), P("fblk", None, None), P())
    out_specs = (P("fblk", None, None), P("tiles", "fblk", None, None))
    return jax.shard_map(body, mesh=mesh, in_specs=in_specs, out_specs=out_specs, check_vma=False)
```

```python
import jax
import jax.numpy as jnp
from jax import lax
from jax.experimental import pallas as pl
from jax.experimental.pallas import tpu as pltpu
from jax.sharding import PartitionSpec as P

STEPS = 4
TAPS = 11
H, W = 48, 128
PIX = H * W
KB = 64
HALF = KB // 2
COLS = 16 * TAPS
PAD = 5 * W
CODE_LANES = 60 * W
SHIFT_LANES = PIX + 2 * PAD
GROUPS = 3
MAP_LANES = 56 * W
CHUNK = 512
ROWS = CHUNK // W
UPPER = H // 2
EARLY = (UPPER - 5) // ROWS

step_filter = 128.0
step_code = 0.05
shrink_level = 0.02
MESH = pl.DeviceIdType.MESH
F32, BF16 = jnp.float32, jnp.bfloat16


def flip(index, mask):
    out = index
    bit = 1
    while bit <= mask:
        if mask & bit:
            out = out + bit * (1 - 2 * ((index // bit) % 2))
        bit *= 2
    return out


def tree_sum(parts):
    while len(parts) > 1:
        parts = [
            parts[i] + parts[i + 1] if i + 1 < len(parts) else parts[i]
            for i in range(0, len(parts), 2)
        ]
    return parts[0]


def nt_dot(a, b):
    return lax.dot_general(a, b, (((1,), (1,)), ((), ())), preferred_element_type=F32)


def kernel(
    plan, images_in, codes_in, filters_in, filters_out, codes_out,
    images, codes, filters, turned_filters, natural, held, maps, spread_mat, expand_mat, shifts, bank, parts, near, far, send, recv, local,
    synth_mat, code_mat, early_grad,
):
    tile, fblk = lax.axis_index("tiles"), lax.axis_index("fblk")
    z_peers = [(n, 0) for n in range(1, 8)]
    xy_peers = [(8 * n, 0) for n in range(1, 8)]
    group_peers = [(0, r) for r in range(1, 4)]
    peers = z_peers + xy_peers + group_peers
    along_z = (z_peers, (4, 3, 5, 6, 2, 7, 1))
    along_xy = (xy_peers, (5, 4, 7, 3, 6, 2, 1))
    in_group = (group_peers, (2, 3, 1))

    farthest_first = [
        group[n - 1] for group, n in [(z_peers, n) for n in along_z[1]] + [(xy_peers, n) for n in along_xy[1]]
        + [(group_peers, n) for n in in_group[1]]
    ]
    places = {peer: (flip(tile, peer[0]), flip(fblk, peer[1])) for peer in peers}

    def device(peer):
        return places[peer]

    barrier = pltpu.get_barrier_semaphore()
    for peer in farthest_first:
        pl.semaphore_signal(barrier, inc=1, device_id=device(peer), device_id_type=MESH)

    loads = [
        pltpu.make_async_copy(codes_in, codes, local.at[0]),
        pltpu.make_async_copy(filters_in, filters, local.at[1]),
        pltpu.make_async_copy(images_in, images, local.at[2]),
    ]
    for load in loads:
        load.start()

    row = lax.broadcasted_iota(jnp.int32, (4 * GROUPS * 16, 128), 0)
    col = lax.broadcasted_iota(jnp.int32, (4 * GROUPS * 16, 128), 1)
    tap = (row + 5) & 15
    for r in range(4):
        first = r * GROUPS * 16
        line = ((row - first) >> 4) * 4 + r
        part = (tap < TAPS) & (line < TAPS) & (line * TAPS + 10 - tap == col)
        spread_mat[first : first + GROUPS * 16, :] = jnp.where(part, 1.0, 0.0).astype(BF16)[
            first : first + GROUPS * 16
        ]
    col = lax.broadcasted_iota(jnp.int32, (128, COLS), 0)
    row = lax.broadcasted_iota(jnp.int32, (128, COLS), 1)
    tap = (row + 5) & 15
    part = (tap < TAPS) & ((row >> 4) * TAPS + tap == col)
    expand_mat[...] = jnp.where(part, 1.0, 0.0).astype(BF16)
    held[:, 0:PAD] = jnp.zeros((KB, PAD), BF16)
    held[:, PAD + PIX : CODE_LANES] = jnp.zeros((KB, CODE_LANES - PAD - PIX), BF16)
    shifts[:, 0:PAD] = jnp.zeros((16, PAD), BF16)
    shifts[:, PAD + PIX : SHIFT_LANES] = jnp.zeros((16, PAD), BF16)
    for load in loads:
        load.wait()
    turned_filters[...] = jnp.zeros((128, 128), F32)
    for a in range(TAPS):
        turned_filters[a * TAPS : (a + 1) * TAPS, 0:KB] = filters[a]
    bank[...] = jnp.transpose(turned_filters[...])[0:KB, :]

    def unfold(k, carry):
        rows = pl.ds(pl.multiple_of(k * 8 * H, 8 * H), 8 * H)
        natural[rows, :] = codes[rows, :].astype(F32)
        return carry

    lax.fori_loop(0, KB // 8, unfold, 0)
    for y in range(H):
        held[:, PAD + y * W : PAD + (y + 1) * W] = natural[pl.ds(y, KB, stride=H), :].astype(BF16)

    tap = (lax.broadcasted_iota(jnp.int32, (16, W), 0) + 5) & 15
    lane = lax.broadcasted_iota(jnp.int32, (16, W), 1)
    source = lane - tap + 5
    inside = (tap < TAPS) & (source >= 0) & (source < W)

    def turn(front, back):
        front = pltpu.roll(front, 0, 1, stride=1, stride_axis=0)
        back = pltpu.roll(back, W - 8, 1, stride=1, stride_axis=0)
        return jnp.where(inside, jnp.concatenate([front, back], axis=0), 0.0)

    def set_synth_mat():
        slabs = nt_dot(spread_mat[...], bank[...].astype(BF16))
        synth_mat[...] = jnp.concatenate(
            [slabs[r * GROUPS * 16 : (r + 1) * GROUPS * 16] for r in range(4)], axis=1
        ).astype(BF16)

    def synth(kind, s, half):
        @pl.when(tile >= 0)
        def _():
            weights = synth_mat[...]
            lag = 3
            middle, end = UPPER // ROWS + lag, H // ROWS + lag
            for c in range(middle) if half == 0 else range(middle, end):
                at = c * CHUNK
                if at < MAP_LANES:
                    piled = jnp.concatenate(
                        [held[:, at + r * W : at + r * W + CHUNK] for r in range(4)], axis=0
                    )
                    maps[:, at : at + CHUNK] = jnp.dot(weights, piled, preferred_element_type=F32)
                if c >= lag:
                    for y in range((c - lag) * ROWS, (c - lag + 1) * ROWS):
                        total = tree_sum([
                            maps[g * 16 : (g + 1) * 16, (y + 4 * g) * W : (y + 4 * g + 1) * W]
                            for g in range(GROUPS)
                        ])
                        turned = turn(total[0:8], total[8:16])
                        parts[kind, s, 0, y : y + 1, :] = jnp.sum(turned, axis=0, keepdims=True)

    def copies(src, dst, q, s, n, peer):
        return pltpu.make_async_remote_copy(
            src_ref=src.at[s, 0], dst_ref=dst.at[s, n],
            send_sem=send.at[q, s], recv_sem=recv.at[q, s],
            device_id=device(peer), device_id_type=MESH,
        )

    def start(ref, q, s, targets):
        for n in targets[1]:
            copies(ref, ref, q, s, n, targets[0][n - 1]).start()

    def finish(ref, sem, q, s, count):
        got = ref.at[s, pl.ds(1, count)]
        pltpu.make_async_copy(got, got, sem.at[q, s]).wait()

    def send_parts(kind, s, half):
        rows = pl.ds(half * UPPER, UPPER)
        for n in in_group[1]:
            pltpu.make_async_remote_copy(
                src_ref=parts.at[kind, s, 0, rows], dst_ref=parts.at[kind, s, n, rows],
                send_sem=send.at[4 + 2 * kind + half, s], recv_sem=recv.at[4 + 2 * kind + half, s],
                device_id=device(group_peers[n - 1]), device_id_type=MESH,
            ).start()

    def finish_parts(sem, kind, s, half):
        got = parts.at[kind, s, pl.ds(1, 3), pl.ds(half * UPPER, UPPER)]
        pltpu.make_async_copy(got, got, sem.at[4 + 2 * kind + half, s]).wait()

    def synth_and_send(kind, s):
        for half in range(2):
            synth(kind, s, half)
            send_parts(kind, s, half)

    def exchange(kind, s, work):
        for half in range(2):
            finish_parts(recv, kind, s, half)

            @pl.when(tile >= 0)
            def _():
                first = half * UPPER
                rows = slice(first, first + UPPER)
                left = tree_sum([parts[kind, s, r, rows] for r in range(4)]) - images[rows, :]
                for y in range(UPPER):
                    line = jnp.broadcast_to(left[y : y + 1, :], (8, W))
                    at = PAD + (first + y) * W
                    shifts[:, at : at + W] = turn(line, line).astype(BF16)
                work(half, range(EARLY) if half == 0 else range(EARLY, PIX // CHUNK))

    def shift_rows(at):
        return jnp.concatenate(
            [shifts[:, at + (10 - a) * W : at + (10 - a) * W + CHUNK] for a in range(TAPS)], axis=0
        )

    def set_code_mat():
        code_mat[...] = jnp.dot(
            bank[...].astype(BF16), expand_mat[...], preferred_element_type=F32
        ).astype(BF16)

    def step(s, carry):
        def to_gradient(half, chunks):
            total = jnp.zeros((KB, COLS), F32) if half == 0 else early_grad[...]
            for c in chunks:
                at = c * CHUNK
                total = total + nt_dot(held[:, PAD + at : PAD + at + CHUNK], shift_rows(at))
            if half == 0:
                early_grad[...] = total
                return
            big = total.astype(BF16)
            rest = total - big.astype(F32)
            mid = rest.astype(BF16)
            small = (rest - mid.astype(F32)).astype(BF16)
            for q in range(2):
                part = slice(q * HALF, (q + 1) * HALF)
                thirds = nt_dot(
                    jnp.concatenate([big[part], mid[part], small[part]], axis=0), expand_mat[...]
                )
                near[q, s, 0] = thirds[0:HALF] + (thirds[HALF : 2 * HALF] + thirds[2 * HALF :])
                start(near.at[q], q, s, (along_z, along_xy)[q])

        synth_and_send(0, s)
        exchange(0, s, to_gradient)

        finish(near.at[1], recv, 1, s, 7)
        far[1, s, 0] = tree_sum([near[1, s, n] for n in range(8)])
        start(far.at[1], 3, s, along_z)
        finish(near.at[0], recv, 0, s, 7)
        far[0, s, 0] = tree_sum([near[0, s, n] for n in range(8)])
        start(far.at[0], 2, s, along_xy)
        for q in range(2):
            finish(far.at[q], recv, 2 + q, s, 7)
        gradient = jnp.concatenate(
            [tree_sum([far[q, s, n] for n in range(8)]) for q in range(2)], axis=0
        )
        old = bank[...]
        values = old - step_filter * gradient / 393216.0
        values = values / jnp.sqrt(jnp.sum(values * values, axis=1, keepdims=True) + 1e-06)
        owner = jnp.full((KB, 128), plan[s], jnp.int32) == jnp.full((KB, 128), fblk, jnp.int32)
        bank[...] = jnp.where(owner, values, old)
        set_synth_mat()
        synth_and_send(1, s)
        pl.when(tile >= 0)(set_code_mat)

        def to_codes(half, chunks):
            weights = code_mat[...]
            for c in chunks:
                at = c * CHUNK
                slope = jnp.dot(weights, shift_rows(at), preferred_element_type=F32)
                value = held[:, PAD + at : PAD + at + CHUNK].astype(F32) - step_code * slope
                value = value - jnp.clip(value, -shrink_level, shrink_level)
                held[:, PAD + at : PAD + at + CHUNK] = value.astype(BF16)

        exchange(1, s, to_codes)
        return carry

    set_synth_mat()
    pl.semaphore_wait(barrier, len(peers))

    lax.fori_loop(0, STEPS, step, 0)
    for y in range(H):
        natural[pl.ds(y, KB, stride=H), :] = held[:, PAD + y * W : PAD + (y + 1) * W].astype(F32)
    for s in range(STEPS):
        for q in range(2):
            finish(near.at[q], send, q, s, 7)
            finish(far.at[q], send, 2 + q, s, 7)
            for half in range(2):
                finish_parts(send, q, s, half)
    turned_filters[0:KB, :] = bank[...]
    turned_filters[...] = jnp.transpose(turned_filters[...])
    for a in range(TAPS):
        filters_out[a] = turned_filters[a * TAPS : (a + 1) * TAPS, 0:KB]

    def fold(k, carry):
        rows = pl.ds(pl.multiple_of(k * 8 * H, 8 * H), 8 * H)
        codes_out[rows, :] = natural[rows, :].astype(BF16)
        return carry

    lax.fori_loop(0, KB // 8, fold, 0)


def body(images, sparse_codes, filters, plan):
    vmem = pl.BlockSpec(memory_space=pltpu.VMEM)
    hbm = pl.BlockSpec(memory_space=pltpu.HBM)
    new_filters, new_codes = pl.pallas_call(
        kernel,
        out_shape=(
            jax.ShapeDtypeStruct((TAPS, TAPS, KB), F32),
            jax.ShapeDtypeStruct((KB * H, W), BF16),
        ),
        in_specs=[pl.BlockSpec(memory_space=pltpu.SMEM), hbm, hbm, hbm],
        out_specs=(vmem, vmem),
        scratch_shapes=[
            pltpu.VMEM((H, W), F32),
            pltpu.VMEM((KB * H, W), BF16),
            pltpu.VMEM((TAPS, TAPS, KB), F32),
            pltpu.VMEM((128, 128), F32),
            pltpu.VMEM((KB * H, W), F32),
            pltpu.VMEM((KB, CODE_LANES), BF16),
            pltpu.VMEM((GROUPS * 16, MAP_LANES), F32),
            pltpu.VMEM((4 * GROUPS * 16, 128), BF16),
            pltpu.VMEM((128, COLS), BF16),
            pltpu.VMEM((16, SHIFT_LANES), BF16),
            pltpu.VMEM((KB, 128), F32),
            pltpu.VMEM((2, STEPS, 4, H, W), F32),
            pltpu.VMEM((2, STEPS, 8, HALF, 128), F32),
            pltpu.VMEM((2, STEPS, 8, HALF, 128), F32),
            pltpu.SemaphoreType.DMA((8, STEPS)),
            pltpu.SemaphoreType.DMA((8, STEPS)),
            pltpu.SemaphoreType.DMA((3,)),
            pltpu.VMEM((GROUPS * 16, 4 * KB), BF16),
            pltpu.VMEM((KB, COLS), BF16),
            pltpu.VMEM((KB, COLS), F32),
        ],
        compiler_params=pltpu.CompilerParams(
            collective_id=0, has_side_effects=True, vmem_limit_bytes=52 * 1024 * 1024 + 512 * 1024
        ),
        name="coordinate_steps",
    )(plan, images.reshape(H, W), sparse_codes.reshape(KB * H, W), filters.transpose(1, 2, 0))
    return (
        new_filters.transpose(2, 0, 1),
        new_codes.reshape(1, KB, H, W),
    )


def solution(mesh):
    in_specs = (P("tiles", None, None), P("tiles", "fblk", None, None), P("fblk", None, None), P())
    out_specs = (P("fblk", None, None), P("tiles", "fblk", None, None))
    return jax.shard_map(body, mesh=mesh, in_specs=in_specs, out_specs=out_specs, check_vma=False)
```
